32 devices in a mesh: src: 16 (over z, y, x), seg: 2 (over core).
Axes of the slice: x: 2, y: 2, z: 4, core: 2. Of those that a mesh axis runs over, the one named last changes fastest.
Arguments:
- spectra: bfloat16 [4096, 2, 2, 2048], P('src', 'seg'), may hold values from -6 to 6
- pairs: int32 [32, 2], P('src'), may hold values from 0 to 15, as said below
- pair_count: int32 [16], P('src'), may hold values from 1 to 2, as said below
Outputs:
- stacks: float32 [32, 256, 1536], P('src', 'seg')
The draws below stay inside these ranges and needn't reach their ends.
Inputs may be any that keep to these rules, and one draw needn't show every extreme that they name: pairs[p] = (i, j) with d <= i <= j <= min(d + 4, 15) where d = p // 2; every owner d with d + 4 < 16 has a slot with j = d + 4. `pair_count`: at least one owner has all 2 slots live.
All inputs are finite; a program needn't handle non-finite values.
Results may differ from the reference program's by a relative error of at most 0.0011.
Values may be sent and summed in bfloat16 or wider, within the bound.
No kernel may reach another device: no remote copies, remote signals or barrier semaphores. Data moves between devices by JAX's collectives and lax.ppermute only.
A program may use at most 128 MiB of HBM per device.

```python
import jax
import jax.numpy as jnp
from jax import lax

F = 2048
BLK = 256
LAGS = 6
REACH = 4
SLOTS = 2
NB = 16
CHANNELS = 4096
HOURS = 2


def draw_pairs(key, part):
    key = jax.random.fold_in(key, 11)
    first_key, second_key = jax.random.split(key)
    total = NB * SLOTS
    slot = jnp.arange(total, dtype=jnp.int32)
    owner = slot // SLOTS
    upper = jnp.minimum(owner + REACH, NB - 1)
    first = jax.random.randint(first_key, (total,), owner, upper + 1)
    second = jax.random.randint(second_key, (total,), first, upper + 1)
    forced = (slot % SLOTS == 0) & (owner + REACH <= NB - 1)
    second = jnp.where(forced, owner + REACH, second)
    return jnp.stack([first, second], axis=1).astype(jnp.int32)


def draw_pair_count(key, part):
    key = jax.random.fold_in(key, 23)
    count_key, pick_key = jax.random.split(key)
    counts = jax.random.randint(count_key, (NB,), 1, SLOTS + 1)
    chosen = jax.random.randint(pick_key, (), 0, NB)
    return counts.at[chosen].set(SLOTS).astype(jnp.int32)


def level_of(own_key, dims, cuts, least, top_value):
    loudness, own = 1.0, jax.random.fold_in(own_key, 6)
    for axis_at, shards_of in cuts:
        draws = jnp.exp(jax.random.uniform(jax.random.fold_in(own, axis_at), (shards_of,), jnp.float32, least / len(cuts), top_value / len(cuts)))
        loudness = loudness * jnp.repeat(draws, dims[axis_at] // shards_of).reshape([-1 if axis == axis_at else 1 for axis in range(len(dims))])
    return loudness


def noise(key, extent, scale, bound, cuts=(), held_as=jnp.bfloat16):
    drawn = jax.random.normal(key, extent, jnp.float32) * scale
    if len(cuts) > 0:
        drawn = level_of(key, extent, cuts, -0.22, 0.18) * drawn
    return jnp.clip(drawn, min=-bound, max=bound).astype(held_as)


def setup_inputs(seed: int = 0) -> dict:
    seeds = jax.random.split(jax.random.key(seed), 4)
    spectra = noise(seeds[0], (CHANNELS, HOURS, 2, F), 1.0, 6.0, ((0, 16), (1, 2)))
    pairs = draw_pairs(jax.random.fold_in(seeds[3], 71), 0)
    pair_count = draw_pair_count(jax.random.fold_in(seeds[3], 71), 0)
    return {"spectra": spectra, "pairs": pairs, "pair_count": pair_count}


def lag_tables():
    freq = jnp.arange(F, dtype=jnp.int32)
    lagval = jnp.arange(LAGS, dtype=jnp.int32) - LAGS // 2
    phase = (lagval[:, None] * freq[None, :]) % (2 * F)
    theta = phase.astype(jnp.float32) * (jnp.pi / F)
    return jnp.cos(theta), jnp.sin(theta)


def build_rotated(block, cosine, sine):
    real_part = block[:, :, 0, :].astype(jnp.float32)[:, None]
    imag_part = block[:, :, 1, :].astype(jnp.float32)[:, None]
    cos_b = cosine[None, :, None, :]
    sin_b = sine[None, :, None, :]
    first = real_part * cos_b - imag_part * sin_b
    second = imag_part * cos_b + real_part * sin_b
    stacked = jnp.stack([first, second], axis=3)
    rows = block.shape[0] * LAGS
    return stacked.reshape(rows, -1).astype(jnp.bfloat16)


def reference(spectra, pairs, pair_count):
    cosine, sine = lag_tables()
    scale = (HOURS * F) ** -0.5

    def one_slot(index):
        owner = index // SLOTS
        first = lax.dynamic_slice_in_dim(spectra, (pairs[index, 0] * BLK).astype(jnp.int32), BLK, 0)
        second = lax.dynamic_slice_in_dim(spectra, (pairs[index, 1] * BLK).astype(jnp.int32), BLK, 0)
        rotated = build_rotated(first, cosine, sine)
        right = second.reshape(BLK, -1)
        prod = lax.dot_general(rotated, right, (((1,), (1,)), ((), ())), preferred_element_type=jnp.float32)
        prod = jnp.transpose(prod.reshape(BLK, LAGS, BLK), (0, 2, 1)).reshape(BLK, BLK * LAGS)
        live = (index % SLOTS) < pair_count[owner]
        return jnp.where(live, prod * scale, jnp.zeros_like(prod))

    return lax.map(one_slot, jnp.arange(NB * SLOTS, dtype=jnp.int32))
```

```python
import functools

import jax
import jax.numpy as jnp
from jax import lax
from jax.experimental import pallas as pl
from jax.experimental.pallas import tpu as pltpu
from jax.sharding import PartitionSpec as P

LAGS = 6
REACH = 4
SLOTS = 2
WINDOW = 6
VMEM = 56 * 1024 * 1024


def routes(axis, move):
    size = lax.axis_size(axis)
    return [(i, move(i)) for i in range(size) if 0 <= move(i) < size]


def to_pair(value):
    return lax.ppermute(value, "src", routes("src", lambda d: d ^ 1))


def to_row(value):
    return lax.ppermute(value, "src", routes("src", lambda d: d ^ 2))


def to_below(value):
    return lax.ppermute(value, "src", routes("src", lambda d: d - REACH))


def lag_tables(freqs, lags):
    freq = jnp.arange(freqs, dtype=jnp.int32)
    lagval = jnp.arange(lags, dtype=jnp.int32) - lags // 2
    phase = lagval[:, None] * freq[None, :] % (2 * freqs)
    theta = phase.astype(jnp.float32) * (jnp.pi / freqs)
    return (jnp.cos(theta), jnp.sin(theta))


def rotate_into(x_ref, real, imag, table, rows, row, cols, half):
    height = real.shape[0]
    other = pl.ds(half + cols, real.shape[1])
    here = pl.ds(cols, real.shape[1])

    def put(lag, first, second):
        at = pl.ds(lag * rows + row, height)
        x_ref[at, here] = first.astype(jnp.bfloat16)
        x_ref[at, other] = second.astype(jnp.bfloat16)

    put(3, real, imag)
    for plus, minus, row_c in ((0, None, 0), (4, 2, 1), (5, 1, 2)):
        cos, sin = table(row_c), table(row_c + 3)
        rc, im_s, ic, rs = real * cos, imag * sin, imag * cos, real * sin
        put(plus, rc - im_s, ic + rs)
        if minus is not None:
            put(minus, rc + im_s, ic - rs)


def corr_kernel(count, meta, table, *refs):
    held = refs[:WINDOW]
    outs = refs[WINDOW : WINDOW + count]
    left, right, x_ref, sems = refs[WINDOW + count :]
    slot, part = pl.program_id(0), pl.program_id(1)
    now = lax.rem(slot, 2)
    slots = pl.num_programs(0)

    def fetch(which, buffer):
        for side, target in ((0, left), (1, right)):
            name = meta[2 * which + side]
            for k in range(WINDOW):

                @pl.when(name == k)
                def _():
                    pltpu.make_async_copy(held[k], target.at[buffer], sems.at[side, buffer]).start()

    @pl.when((slot == 0) & (part == 0))
    def _():
        fetch(0, 0)

    @pl.when(part == 0)
    def _():
        @pl.when(slot + 1 < slots)
        def _():
            fetch(slot + 1, 1 - now)

        for side, target in ((0, left), (1, right)):
            pltpu.make_async_copy(held[0], target.at[now], sems.at[side, now]).wait()

    rows = outs[0].shape[2]
    half = left.shape[2] // 2
    seg = lax.rem(meta[2 * slots] + part, count)
    wide, high = 256, 16

    for cols in range(0, half, wide):
        def step(at, carry):
            src = pl.ds(pl.multiple_of(seg * rows + at * high, high), high)
            real = left[now, src, pl.ds(cols, wide)].astype(jnp.float32)
            imag = left[now, src, pl.ds(half + cols, wide)].astype(jnp.float32)
            look = lambda r: table[pl.ds(r, 1), pl.ds(cols, wide)]
            rotate_into(x_ref, real, imag, look, rows, pl.multiple_of(at * high, high), cols, half)
            return carry

        lax.fori_loop(0, rows // high, step, 0, unroll=True)

    product = lax.dot_general(
        x_ref[...], right[now], (((1,), (1,)), ((), ())), preferred_element_type=jnp.float32
    )
    for k in range(count):

        @pl.when(part == k)
        def _():
            outs[k][0] = product.reshape(LAGS, rows, right.shape[1])


def correlate(meta, table, held, count, slots):
    height, width = held[0].shape
    rows = height // count
    shape = jax.ShapeDtypeStruct((slots, LAGS, rows, height), jnp.float32)
    return pl.pallas_call(
        functools.partial(corr_kernel, count),
        out_shape=[shape] * count,
        grid=(slots, count),
        in_specs=[pl.BlockSpec(memory_space=pltpu.SMEM), pl.BlockSpec(memory_space=pltpu.VMEM)]
        + [pl.BlockSpec(memory_space=pl.ANY)] * WINDOW,
        out_specs=[pl.BlockSpec((1, LAGS, rows, height), lambda s, k: (s, 0, 0, 0))] * count,
        scratch_shapes=[
            pltpu.VMEM((2, height, width), jnp.bfloat16),
            pltpu.VMEM((2, height, width), jnp.bfloat16),
            pltpu.VMEM((LAGS * rows, width), jnp.bfloat16),
            pltpu.SemaphoreType.DMA((2, 2)),
        ],
        compiler_params=pltpu.CompilerParams(vmem_limit_bytes=VMEM),
        cost_estimate=pl.CostEstimate(
            flops=2 * slots * LAGS * height * height * width, bytes_accessed=4 * slots * height * width, transcendentals=0
        ),
    )(meta, table, *held)


def finish_kernel(count, scale, live, spread, *refs):
    parts, out = refs[: count + 1], refs[count + 1]
    slot = pl.program_id(0)
    rows, width = parts[0].shape[2], parts[0].shape[3]
    step = spread.shape[0] // LAGS
    high, low = [], []
    for at in range(0, width, step):
        lags = []
        for lag in range(LAGS):
            total = parts[0][0, lag, :, at : at + step]
            for part in parts[1:]:
                total = total + part[0, lag, :, at : at + step]
            lags.append(total)
        total = jnp.concatenate(lags, axis=1)
        top = total.astype(jnp.bfloat16)
        high.append(top)
        low.append((total - top.astype(jnp.float32)).astype(jnp.bfloat16))
    stacked = jnp.concatenate(high + low, axis=0)
    moved = jnp.dot(stacked, spread[...], preferred_element_type=jnp.float32)
    keep = live[slot] > 0
    for k in range(width // step):
        both = moved[k * rows : (k + 1) * rows] + moved[(k + width // step) * rows : (k + width // step + 1) * rows]
        out[0, :, k * step * LAGS : (k + 1) * step * LAGS] = jnp.where(keep, both * scale, jnp.zeros_like(both))


def finish(live, parts, scale):
    slots, _, rows, width = parts[-1].shape
    step = min(128, width)
    lag_of, chan_of = jnp.arange(LAGS * step) // step, jnp.arange(LAGS * step) % step
    spread = (jnp.arange(LAGS * step)[None, :] == (chan_of * LAGS + lag_of)[:, None]).astype(jnp.bfloat16)
    return pl.pallas_call(
        functools.partial(finish_kernel, len(parts) - 1, scale),
        out_shape=jax.ShapeDtypeStruct((slots, rows, width * LAGS), jnp.float32),
        grid=(slots,),
        in_specs=[pl.BlockSpec(memory_space=pltpu.SMEM), pl.BlockSpec(memory_space=pltpu.VMEM)]
        + [pl.BlockSpec((1, LAGS, rows, width), lambda s: (s, 0, 0, 0))] * len(parts),
        out_specs=pl.BlockSpec((1, rows, width * LAGS), lambda s: (s, 0, 0)),
        compiler_params=pltpu.CompilerParams(vmem_limit_bytes=VMEM),
    )(live, spread, *parts)


def shards(spectra, pairs, pair_count):
    blk, freqs = spectra.shape[0], spectra.shape[3]
    half = freqs // 2
    count = lax.axis_size("seg")
    me = lax.axis_index("src")
    seg = lax.axis_index("seg")
    side, row = me & 1, (me >> 1) & 1
    slots = pairs.shape[0]

    cosine, sine = lag_tables(freqs, LAGS)
    rows = jnp.array([0, 4, 5])
    table = jnp.concatenate([cosine[rows], sine[rows], cosine[rows][:2]], axis=0)
    table = lax.dynamic_slice_in_dim(table, side * half, half, 1)
    named = jnp.concatenate([pairs, to_pair(pairs)], axis=0) - (me & ~1)
    local = (named & ~1) + ((named & 1) ^ side)
    meta = jnp.concatenate([local.reshape(-1), seg[None]]).astype(jnp.int32)
    live = (jnp.arange(slots) < pair_count[0]).astype(jnp.int32)

    halves = spectra[:, 0].reshape(blk, 2, 2, half)
    mine = lax.dynamic_index_in_dim(halves, side, 2, keepdims=False).reshape(blk, 2 * half)
    theirs = lax.dynamic_index_in_dim(halves, 1 - side, 2, keepdims=False).reshape(blk, 2 * half)

    cuts = 4
    held = []
    for cut in range(cuts):
        span = slice(cut * blk // cuts, (cut + 1) * blk // cuts)
        own = mine[span]
        swapped = to_pair(theirs[span])
        above, above_swapped = to_below(own), to_below(swapped)
        beside = to_row(jnp.where(row == 1, own, above))
        beside_swapped = to_row(jnp.where(row == 1, swapped, above_swapped))
        held.append((own, swapped, beside, beside_swapped, above, above_swapped))
    held = [mine] + [jnp.concatenate([h[k] for h in held], axis=0) for k in range(1, WINDOW)]

    shares = correlate(meta, table, held, count, 2 * slots)
    parts = [shares[0]]
    for k in range(1, count):
        parts.append(lax.ppermute(shares[k], "seg", routes("seg", lambda i: (i + k) % count)))
    other = sum(p[slots:] for p in parts)
    own = [p[:slots] for p in parts] + [to_pair(other)]
    scale = float(count * spectra.shape[1] * freqs) ** (-0.5)
    return finish(live, own, scale)


def solution(mesh):
    in_specs = (P("src", "seg", None, None), P("src", None), P("src"))
    out_specs = P("src", "seg", None)
    return jax.shard_map(shards, mesh=mesh, in_specs=in_specs, out_specs=out_specs, check_vma=False)
```

```python
import functools

import jax
import jax.numpy as jnp
from jax import lax
from jax.experimental import pallas as pl
from jax.experimental.pallas import tpu as pltpu
from jax.sharding import PartitionSpec as P

LAGS = 6
REACH = 4
SLOTS = 2
WINDOW = 6
LANES = 128
VMEM = 56 * 1024 * 1024


def routes(axis, move):
    size = lax.axis_size(axis)
    return [(i, move(i)) for i in range(size) if 0 <= move(i) < size]


def to_pair(value):
    return lax.ppermute(value, "src", routes("src", lambda d: d ^ 1))


def to_row(value):
    return lax.ppermute(value, "src", routes("src", lambda d: d ^ 2))


def to_site(value):
    size = lax.axis_size("src")
    return lax.ppermute(value, "src", routes("src", lambda d: (d + REACH) % size if d >> 1 & 1 else d - REACH))


def to_partner_site(value):
    size = lax.axis_size("src")
    return lax.ppermute(value, "src", routes("src", lambda d: ((d + REACH) % size if d >> 1 & 1 else d) ^ 1))


def to_owner(value):
    size = lax.axis_size("src")
    return lax.ppermute(value, "src", routes("src", lambda d: (d - REACH) % size if d >> 1 & 1 else -1))


def lag_tables(freqs, lags):
    freq = jnp.arange(freqs, dtype=jnp.int32)
    lagval = jnp.arange(lags, dtype=jnp.int32) - lags // 2
    phase = lagval[:, None] * freq[None, :] % (2 * freqs)
    theta = phase.astype(jnp.float32) * (jnp.pi / freqs)
    return (jnp.cos(theta), jnp.sin(theta))


def rotate_into(x_ref, real, imag, table, rows, row, cols, half):
    height = real.shape[0]
    other = pl.ds(half + cols, real.shape[1])
    here = pl.ds(cols, real.shape[1])

    def put(lag, first, second):
        at = pl.ds(lag * rows + row, height)
        x_ref[at, here] = first.astype(jnp.bfloat16)
        x_ref[at, other] = second.astype(jnp.bfloat16)

    put(3, real, imag)
    for plus, minus, row_c in ((0, None, 0), (4, 2, 1), (5, 1, 2)):
        cos, sin = table(row_c), table(row_c + 3)
        rc, im_s, ic, rs = real * cos, imag * sin, imag * cos, real * sin
        put(plus, rc - im_s, ic + rs)
        if minus is not None:
            put(minus, rc + im_s, ic - rs)


def stage_tiles(stage):
    return [(a, stage) for a in range(stage)] + [(stage, b) for b in range(stage + 1)]


def corr_kernel(count, stage, first, sets, layout, meta, table, *refs):
    parts = stage + 1
    arrays = 1 + max(item[0] for items in layout for item in items)
    blocks, outs = refs[:arrays], refs[arrays:-4]
    left, right, x_ref, sems = refs[-4:]
    at = pl.program_id(0)
    now = lax.rem(at, 2)
    half = left.shape[3]
    size = left.shape[2] // parts
    piece = size // count

    def copy(item, buffer, p, side):
        ref, source, start, rows = item
        span = pl.ds(start, rows)
        target = left.at[buffer, p, span] if side == 0 else right.at[buffer, span, pl.ds(p * half, half)]
        return pltpu.make_async_copy(blocks[ref].at[p, pl.ds(source, rows)], target, sems.at[side, buffer])

    def fetch(which, buffer):
        for side in range(2):
            name = meta[2 * (first + which) + side]
            for k, items in enumerate(layout):

                @pl.when(name == k)
                def _():
                    for item in items:
                        for p in range(2):
                            copy(item, buffer, p, side).start()

    @pl.when(at == 0)
    def _():
        fetch(0, 0)

    @pl.when(at + 1 < pl.num_programs(0))
    def _():
        fetch(at + 1, 1 - now)

    for side in range(2):
        target = left.at[now] if side == 0 else right.at[now]
        pltpu.make_async_copy(target, target, sems.at[side, now]).wait()

    wide, high = 256, 16
    for c in range(parts):
        for k in range(count):
            base = c * size + lax.rem(meta[8] + k, count) * piece
            block = (c * count + k) * LAGS * piece
            for cols in range(0, half, wide):
                for step in range(0, piece, high):
                    src = pl.ds(pl.multiple_of(base + step, high), high)
                    real = left[now, 0, src, pl.ds(cols, wide)].astype(jnp.float32)
                    imag = left[now, 1, src, pl.ds(cols, wide)].astype(jnp.float32)
                    look = lambda r: table[pl.ds(r, 1), pl.ds(cols, wide)]
                    rotate_into(x_ref, real, imag, look, piece, block + step, cols, half)
    product = lax.dot_general(
        x_ref[...], right[now], (((1,), (1,)), ((), ())), preferred_element_type=jnp.float32
    )
    for n, tiles in enumerate(sets):

        @pl.when(at // SLOTS == n)
        def _():
            for k in range(count):
                for tile, (a, b) in enumerate(tiles):
                    block = (a * count + k) * LAGS * piece
                    out = product[block : block + LAGS * piece, b * size : (b + 1) * size]
                    outs[n * count + k][0, :, tile * piece : (tile + 1) * piece] = out.reshape(LAGS, piece, size)


def correlate(meta, table, sources, count, stage, width, first, sets):
    size, half, parts = width, sources[0][0][0].shape[2], stage + 1
    piece = size // count
    layout, blocks = [], []
    for spans in sources:
        items, start = [], 0
        for array, source, rows in spans:
            rows = min(rows, parts * size - start)
            if rows > 0:
                if not any(array is block for block in blocks):
                    blocks.append(array)
                at = [array is block for block in blocks].index(True)
                items.append((at, source, start, rows))
                start += rows
        layout.append(tuple(items))
    shapes = [(SLOTS, LAGS, len(tiles) * piece, size) for tiles in sets for _ in range(count)]
    outs = pl.pallas_call(
        functools.partial(corr_kernel, count, stage, first, sets, tuple(layout)),
        out_shape=[jax.ShapeDtypeStruct(shape, jnp.float32) for shape in shapes],
        grid=(SLOTS * len(sets),),
        in_specs=[pl.BlockSpec(memory_space=pltpu.SMEM), pl.BlockSpec(memory_space=pltpu.VMEM)]
        + [pl.BlockSpec(memory_space=pl.ANY)] * len(blocks),
        out_specs=[
            pl.BlockSpec((1,) + shape[1:], lambda s, n=n // count: (jnp.clip(s - n * SLOTS, 0, SLOTS - 1), 0, 0, 0))
            for n, shape in enumerate(shapes)
        ],
        scratch_shapes=[
            pltpu.VMEM((2, 2, parts * size, half), jnp.bfloat16),
            pltpu.VMEM((2, parts * size, 2 * half), jnp.bfloat16),
            pltpu.VMEM((parts * LAGS * size, 2 * half), jnp.bfloat16),
            pltpu.SemaphoreType.DMA((2, 2)),
        ],
        compiler_params=pltpu.CompilerParams(vmem_limit_bytes=VMEM),
        cost_estimate=pl.CostEstimate(flops=10**13, bytes_accessed=10**10, transcendentals=0),
    )(meta, table, *blocks)
    return [outs[n * count : (n + 1) * count] for n in range(len(sets))]


def finish_kernel(count, piece, stages, slot, scale, layout, meta, spread, *refs):
    out = refs[-1]
    away = meta[0] > 0

    def find(stage, lag, at):
        ref, first = layout[stage][lag]
        return jnp.where(away, refs[2 * ref + 1][0, lag - first, at], refs[2 * ref][0, lag - first, at])

    tiles = [(stage, t, a, b) for stage in range(stages) for t, (a, b) in enumerate(stage_tiles(stage))]
    high, low = [], []
    for stage, t, _, _ in tiles:
        at = slice(t * piece, (t + 1) * piece)
        total = jnp.concatenate([find(stage, lag, at) for lag in range(LAGS)], axis=1)
        top = total.astype(jnp.bfloat16)
        high.append(top)
        low.append((total - top.astype(jnp.float32)).astype(jnp.bfloat16))
    moved = jnp.dot(jnp.concatenate(high + low, axis=0), spread[...], preferred_element_type=jnp.float32)
    keep = slot < meta[1]
    run = piece * LAGS
    for n, (_, _, a, b) in enumerate(tiles):
        m = n + len(tiles)
        both = (moved[n * piece : (n + 1) * piece] + moved[m * piece : (m + 1) * piece]) * scale
        both = jnp.where(keep, both, jnp.zeros_like(both))
        for seg in range(count):
            col = (seg * stages + b) * run
            out[0, a * piece : (a + 1) * piece, col : col + run] = both[:, seg * run : (seg + 1) * run]


def finish(meta, spread, stacks, slot, count, piece, scale, result):
    layout, arrays = [], []
    for pieces in stacks:
        where = []
        for first, here, back in pieces:
            where += [(len(arrays) // 2, first)] * here.shape[1]
            arrays += [here, back]
        layout.append(tuple(where))
    stages = len(stacks)
    shape = (SLOTS, stages * piece, stages * piece * count * LAGS)
    specs = [pl.BlockSpec((1,) + x.shape[1:], lambda i, at=min(slot, x.shape[0] - 1): (at, 0, 0, 0)) for x in arrays]
    more = [] if result is None else [result]
    return pl.pallas_call(
        functools.partial(finish_kernel, count, piece, stages, slot, scale, tuple(layout)),
        out_shape=jax.ShapeDtypeStruct(shape, jnp.float32),
        grid=(1,),
        in_specs=[pl.BlockSpec(memory_space=pltpu.SMEM), pl.BlockSpec(memory_space=pltpu.VMEM)]
        + specs
        + [pl.BlockSpec(memory_space=pl.ANY)] * len(more),
        out_specs=pl.BlockSpec((1,) + shape[1:], lambda i: (slot, 0, 0)),
        input_output_aliases={2 + len(arrays): 0} if more else {},
        compiler_params=pltpu.CompilerParams(vmem_limit_bytes=VMEM),
        cost_estimate=pl.CostEstimate(flops=1, bytes_accessed=1, transcendentals=0),
    )(meta, spread, *arrays, *more)


def after(value, *done):
    return lax.optimization_barrier((value, *done))[0] if done else value


def over_segments(shares, count):
    parts = [shares[0]]
    for k in range(1, count):
        parts.append(lax.ppermute(shares[k], "seg", routes("seg", lambda i: (i + k) % count)))
    return parts


def shards(spectra, pairs, pair_count):
    blk, freqs = spectra.shape[0], spectra.shape[3]
    half = freqs // 2
    count = lax.axis_size("seg")
    me = lax.axis_index("src")
    seg = lax.axis_index("seg")
    side, row = me & 1, (me >> 1) & 1
    stages = 2
    width = blk // stages
    piece = width // count

    rows = spectra.reshape(count, stages, piece, 2, freqs).transpose(3, 1, 0, 2, 4).reshape(2, blk, freqs)
    rows = lax.optimization_barrier(rows)
    own, theirs = [lax.dynamic_slice_in_dim(rows, which * half, half, 2) for which in (side, 1 - side)]

    with jax.named_scope("pairs_along"):
        site_pairs = jnp.where(row == 1, to_site(pairs), pairs)
    with jax.named_scope("pairs_across"):
        named = jnp.concatenate([to_partner_site(pairs), site_pairs], axis=0)
    own, named = lax.optimization_barrier((own, named))

    sources = [[] for _ in range(WINDOW)]
    swapped, beside, along = [], [], []
    for c in range(stages):
        with jax.named_scope(f"swap{c}"):
            swapped.append(to_pair(after(theirs[:, c * width : (c + 1) * width], *swapped)))
    for c in range(stages):
        for kind in range(2):
            block = (own[:, c * width : (c + 1) * width], swapped[c])[kind]
            with jax.named_scope(f"along_{kind}_{c}"):
                along.append(to_site(after(block, *along[-2:-1])))
            with jax.named_scope(f"beside_{kind}_{c}"):
                beside.append(to_row(after(block, *beside[-2:-1])))
            for group, array in enumerate((block, beside[-1], along[-1])):
                sources[2 * group + kind].append((array, 0, width))

    owners = lax.axis_size("src")
    owner = jnp.where(row == 1, (me + owners - REACH) % owners, me)
    named = jnp.clip(named - (owner & ~1), 0, WINDOW - 1)
    group = jnp.where(row == 1, 2 - (named >> 1), named >> 1)
    meta = jnp.concatenate([(2 * group + ((named & 1) ^ side)).reshape(-1), seg[None]]).astype(jnp.int32)

    cosine, sine = lag_tables(freqs, LAGS)
    table = jnp.concatenate([part[at : at + 1] for part in (cosine, sine) for at in (0, 4, 5)] + [cosine[:2]], axis=0)
    table = lax.dynamic_slice_in_dim(table, side * half, half, 1)

    here, back = [], []

    def over_all(shares, name):
        with jax.named_scope(f"segments_{name}"):
            return sum(over_segments(shares, count))

    def exchange(total, name):
        with jax.named_scope(f"partner_stacks_{name}"):
            return to_pair(total)

    def give_back(mine, came, name):
        total = mine + came
        with jax.named_scope(f"stacks_back_{name}"):
            return total, to_owner(total)

    (partner,) = correlate(meta, table, sources, count, 0, width, 0, (stage_tiles(0),))
    sent = over_all(partner, "0")
    came = [exchange(sent, "0")]
    meta = after(meta, sent)
    every = stage_tiles(0) + stage_tiles(1)
    partner, mine = correlate(meta, table, sources, count, 1, width, 0, (stage_tiles(1), every))
    total = over_all([after(x, came[0]) for x in partner], "1")
    lag_parts = ((0, LAGS // 2), (LAGS // 2, LAGS))
    pieces = [(slot, *lags) for slot in range(SLOTS) for lags in lag_parts]
    came += [exchange(total[slot : slot + 1, low:high], f"1_{slot}_{low}") for slot, low, high in pieces]
    mine = over_all([after(x, total) for x in mine], "own")
    place = jnp.arange(LAGS * width)
    spread = (place[None, :] == (place % width * LAGS + place // width)[:, None]).astype(jnp.bfloat16)
    scale = float(count * spectra.shape[1] * freqs) ** (-0.5)
    meta = jnp.stack([row, pair_count[0]]).astype(jnp.int32)
    first = give_back(mine[:, :, :piece], came[0], "0")
    last = []
    for (slot, low, high), stacks in zip(pieces, came[1:]):
        mine = after(mine, first[0] if not last else last[-1][1])
        last.append((low, *give_back(mine[slot : slot + 1, low:high, piece:], stacks, f"1_{slot}_{low}")))
    result = None
    for slot in range(SLOTS):
        stacks = [[(0, *first)], last[slot * len(lag_parts) : (slot + 1) * len(lag_parts)]]
        result = finish(meta, spread, stacks, slot, count, piece, scale, result)
    return result


def solution(mesh):
    in_specs = (P("src", "seg", None, None), P("src", None), P("src"))
    out_specs = P("src", "seg", None)
    return jax.shard_map(shards, mesh=mesh, in_specs=in_specs, out_specs=out_specs, check_vma=False)
```

```python
import functools

import jax
import jax.numpy as jnp
from jax import lax
from jax.experimental import pallas as pl
from jax.experimental.pallas import tpu as pltpu
from jax.sharding import PartitionSpec as P

LAGS = 6
REACH = 4
SLOTS = 2
WINDOW = 6
LANES = 128
VMEM = 56 * 1024 * 1024


def routes(axis, move):
    size = lax.axis_size(axis)
    return [(i, move(i)) for i in range(size) if 0 <= move(i) < size]


def to_pair(value):
    return lax.ppermute(value, "src", routes("src", lambda d: d ^ 1))


def to_row(value):
    return lax.ppermute(value, "src", routes("src", lambda d: d ^ 2))


def to_below(value):
    return lax.ppermute(value, "src", routes("src", lambda d: d - REACH))


def lag_tables(freqs, lags):
    freq = jnp.arange(freqs, dtype=jnp.int32)
    lagval = jnp.arange(lags, dtype=jnp.int32) - lags // 2
    phase = lagval[:, None] * freq[None, :] % (2 * freqs)
    theta = phase.astype(jnp.float32) * (jnp.pi / freqs)
    return (jnp.cos(theta), jnp.sin(theta))


def rotate_into(x_ref, real, imag, table, rows, row, cols, half):
    height = real.shape[0]
    other = pl.ds(half + cols, real.shape[1])
    here = pl.ds(cols, real.shape[1])

    def put(lag, first, second):
        at = pl.ds(lag * rows + row, height)
        x_ref[at, here] = first.astype(jnp.bfloat16)
        x_ref[at, other] = second.astype(jnp.bfloat16)

    put(3, real, imag)
    for plus, minus, row_c in ((0, None, 0), (4, 2, 1), (5, 1, 2)):
        cos, sin = table(row_c), table(row_c + 3)
        rc, im_s, ic, rs = real * cos, imag * sin, imag * cos, real * sin
        put(plus, rc - im_s, ic + rs)
        if minus is not None:
            put(minus, rc + im_s, ic - rs)


def stage_tiles(stage):
    return [(a, stage) for a in range(stage)] + [(stage, b) for b in range(stage + 1)]


def corr_kernel(count, stage, first, sets, layout, meta, table, *refs):
    parts = stage + 1
    arrays = 1 + max(item[0] for items in layout for item in items)
    blocks, outs = refs[:arrays], refs[arrays:-4]
    left, right, x_ref, sems = refs[-4:]
    at = pl.program_id(0)
    now = lax.rem(at, 2)
    half = left.shape[3]
    size = left.shape[2] // parts
    piece = size // count

    def copy(item, buffer, p, side):
        ref, source, start, rows = item
        span = pl.ds(start, rows)
        target = left.at[buffer, p, span] if side == 0 else right.at[buffer, span, pl.ds(p * half, half)]
        return pltpu.make_async_copy(blocks[ref].at[p, pl.ds(source, rows)], target, sems.at[side, buffer])

    def fetch(which, buffer):
        for side in range(2):
            name = meta[2 * (first + which) + side]
            for k, items in enumerate(layout):

                @pl.when(name == k)
                def _():
                    for item in items:
                        for p in range(2):
                            copy(item, buffer, p, side).start()

    @pl.when(at == 0)
    def _():
        fetch(0, 0)

    @pl.when(at + 1 < pl.num_programs(0))
    def _():
        fetch(at + 1, 1 - now)

    for side in range(2):
        target = left.at[now] if side == 0 else right.at[now]
        pltpu.make_async_copy(target, target, sems.at[side, now]).wait()

    wide, high = 256, 16
    for c in range(parts):
        for k in range(count):
            base = c * size + lax.rem(meta[8] + k, count) * piece
            block = (c * count + k) * LAGS * piece
            for cols in range(0, half, wide):
                for step in range(0, piece, high):
                    src = pl.ds(pl.multiple_of(base + step, high), high)
                    real = left[now, 0, src, pl.ds(cols, wide)].astype(jnp.float32)
                    imag = left[now, 1, src, pl.ds(cols, wide)].astype(jnp.float32)
                    look = lambda r: table[pl.ds(r, 1), pl.ds(cols, wide)]
                    rotate_into(x_ref, real, imag, look, piece, block + step, cols, half)
    product = lax.dot_general(
        x_ref[...], right[now], (((1,), (1,)), ((), ())), preferred_element_type=jnp.float32
    )
    for n, (which, slot, tiles) in enumerate(sets):

        @pl.when((at // SLOTS == which) if slot is None else (at == which * SLOTS + slot))
        def _():
            for k in range(count):
                for tile, (a, b) in enumerate(tiles):
                    block = (a * count + k) * LAGS * piece
                    out = product[block : block + LAGS * piece, b * size : (b + 1) * size]
                    outs[n * count + k][0, :, tile * piece : (tile + 1) * piece] = out.reshape(LAGS, piece, size)


def correlate(meta, table, sources, count, stage, width, first, sets):
    size, half, parts = width, sources[0][0][0].shape[2], stage + 1
    piece = size // count
    layout, blocks = [], []
    for spans in sources:
        items, start = [], 0
        for array, source, rows in spans:
            rows = min(rows, parts * size - start)
            if rows > 0:
                if not any(array is block for block in blocks):
                    blocks.append(array)
                at = [array is block for block in blocks].index(True)
                items.append((at, source, start, rows))
                start += rows
        layout.append(tuple(items))
    shapes = [
        (SLOTS if slot is None else 1, LAGS, len(tiles) * piece, size) for _, slot, tiles in sets for _ in range(count)
    ]
    steps = SLOTS * (1 + max(which for which, _, _ in sets))
    outs = pl.pallas_call(
        functools.partial(corr_kernel, count, stage, first, sets, tuple(layout)),
        out_shape=[jax.ShapeDtypeStruct(shape, jnp.float32) for shape in shapes],
        grid=(steps,),
        in_specs=[pl.BlockSpec(memory_space=pltpu.SMEM), pl.BlockSpec(memory_space=pltpu.VMEM)]
        + [pl.BlockSpec(memory_space=pl.ANY)] * len(blocks),
        out_specs=[
            pl.BlockSpec((1,) + shape[1:], lambda s, n=sets[n // count][0], top=shape[0] - 1: (jnp.clip(s - n * SLOTS, 0, top), 0, 0, 0))
            for n, shape in enumerate(shapes)
        ],
        scratch_shapes=[
            pltpu.VMEM((2, 2, parts * size, half), jnp.bfloat16),
            pltpu.VMEM((2, parts * size, 2 * half), jnp.bfloat16),
            pltpu.VMEM((parts * LAGS * size, 2 * half), jnp.bfloat16),
            pltpu.SemaphoreType.DMA((2, 2)),
        ],
        compiler_params=pltpu.CompilerParams(vmem_limit_bytes=VMEM),
        cost_estimate=pl.CostEstimate(flops=10**13, bytes_accessed=10**10, transcendentals=0),
    )(meta, table, *blocks)
    return [outs[n * count : (n + 1) * count] for n in range(len(sets))]


def finish_kernel(count, piece, stages, slot, scale, pair_count, spread, *refs):
    out = refs[-1]
    tiles = [(stage, t, a, b) for stage in range(stages) for t, (a, b) in enumerate(stage_tiles(stage))]
    own, came = refs[: len(tiles)], refs[len(tiles) : len(tiles) + stages]
    high, low = [], []
    for n, (stage, t, _, _) in enumerate(tiles):
        at = slice(t * piece, (t + 1) * piece)
        total = jnp.concatenate([own[n][0, lag] + came[stage][0, lag, at] for lag in range(LAGS)], axis=1)
        top = total.astype(jnp.bfloat16)
        high.append(top)
        low.append((total - top.astype(jnp.float32)).astype(jnp.bfloat16))
    moved = jnp.dot(jnp.concatenate(high + low, axis=0), spread[...], preferred_element_type=jnp.float32)
    keep = slot < pair_count[0]
    run = piece * LAGS
    for n, (_, _, a, b) in enumerate(tiles):
        m = n + len(tiles)
        both = (moved[n * piece : (n + 1) * piece] + moved[m * piece : (m + 1) * piece]) * scale
        both = jnp.where(keep, both, jnp.zeros_like(both))
        for seg in range(count):
            col = (seg * stages + b) * run
            out[0, a * piece : (a + 1) * piece, col : col + run] = both[:, seg * run : (seg + 1) * run]


def finish(pair_count, spread, own, came, slot, count, piece, scale, result):
    stages = len(came)
    arrays = [*own, *came]
    shape = (SLOTS, stages * piece, stages * piece * count * LAGS)
    specs = [pl.BlockSpec((1,) + x.shape[1:], lambda i, at=min(slot, x.shape[0] - 1): (at, 0, 0, 0)) for x in arrays]
    more = [] if result is None else [result]
    return pl.pallas_call(
        functools.partial(finish_kernel, count, piece, stages, slot, scale),
        out_shape=jax.ShapeDtypeStruct(shape, jnp.float32),
        grid=(1,),
        in_specs=[pl.BlockSpec(memory_space=pltpu.SMEM), pl.BlockSpec(memory_space=pltpu.VMEM)]
        + specs
        + [pl.BlockSpec(memory_space=pl.ANY)] * len(more),
        out_specs=pl.BlockSpec((1,) + shape[1:], lambda i: (slot, 0, 0)),
        input_output_aliases={2 + len(arrays): 0} if more else {},
        compiler_params=pltpu.CompilerParams(vmem_limit_bytes=VMEM),
        cost_estimate=pl.CostEstimate(flops=1, bytes_accessed=1, transcendentals=0),
    )(pair_count, spread, *arrays, *more)


def after(value, *done):
    return lax.optimization_barrier((value, *done))[0] if done else value


def over_segments(shares, count):
    parts = [shares[0]]
    for k in range(1, count):
        parts.append(lax.ppermute(shares[k], "seg", routes("seg", lambda i: (i + k) % count)))
    return parts


def shards(spectra, pairs, pair_count):
    blk, freqs = spectra.shape[0], spectra.shape[3]
    half = freqs // 2
    count = lax.axis_size("seg")
    me = lax.axis_index("src")
    seg = lax.axis_index("seg")
    side, row = me & 1, (me >> 1) & 1
    stages = 2
    width = blk // stages
    piece = width // count

    rows = spectra.reshape(count, stages, piece, 2, freqs).transpose(3, 1, 0, 2, 4).reshape(2, blk, freqs)
    rows = lax.optimization_barrier(rows)
    own, theirs = [lax.dynamic_slice_in_dim(rows, which * half, half, 2) for which in (side, 1 - side)]

    sources = [[] for _ in range(WINDOW)]
    along, beside = [], []
    with jax.named_scope("swap"):
        swapped = [to_pair(theirs[:, c * width : (c + 1) * width]) for c in range(stages)]
    for c in range(stages):
        for kind in range(2):
            block = (own[:, c * width : (c + 1) * width], swapped[c])[kind]
            with jax.named_scope(f"along_{kind}_{c}"):
                along.append(to_below(after(block, *along[-2:-1])))
            if len(along) == 2:
                with jax.named_scope("pairs"):
                    named = to_pair(after(pairs, along[1]))
            with jax.named_scope(f"beside_{kind}_{c}"):
                beside.append(to_row(after(jnp.where(row == 1, block, along[-1]), *beside[-2:-1])))
            for group, array in enumerate((block, beside[-1], along[-1])):
                sources[2 * group + kind].append((array, 0, width))

    named = jnp.clip(jnp.concatenate([named, pairs], axis=0) - (me & ~1), 0, WINDOW - 1)
    local = 2 * (named >> 1) + ((named & 1) ^ side)
    meta = jnp.concatenate([local.reshape(-1), seg[None]]).astype(jnp.int32)
    meta = after(meta, along[-1])

    cosine, sine = lag_tables(freqs, LAGS)
    table = jnp.concatenate([part[at : at + 1] for part in (cosine, sine) for at in (0, 4, 5)] + [cosine[:2]], axis=0)
    table = lax.dynamic_slice_in_dim(table, side * half, half, 1)

    here, back = [], []

    def over_all(shares, name):
        with jax.named_scope(f"segments_{name}"):
            return sum(over_segments(shares, count))

    def exchange(total, name):
        with jax.named_scope(f"partner_stacks_{name}"):
            return to_pair(total)

    (partner,) = correlate(meta, table, sources, count, 0, width, 0, ((0, None, stage_tiles(0)),))
    total = over_all(partner, "0")
    came = [exchange(total, "0")]
    meta = after(meta, total)
    tiles = stage_tiles(1)
    groups = correlate(meta, table, sources, count, 1, width, 0, tuple((0, slot, tiles) for slot in range(SLOTS)))
    totals = [over_all([after(x, came[0]) for x in shares], f"1_{slot}") for slot, shares in enumerate(groups)]
    came.append(exchange(totals[0], "1_0"))
    meta = after(meta, *totals)
    tiles = stage_tiles(0) + tiles
    groups = correlate(meta, table, sources, count, 1, width, SLOTS, tuple((0, None, (tile,)) for tile in tiles))
    for slot in range(1, SLOTS):
        came.append(exchange(after(totals[slot], came[-1], groups[0][0]), f"1_{slot}"))
    mine = [over_all(shares, f"own_{n}") for n, shares in enumerate(groups)]
    place = jnp.arange(LAGS * width)
    spread = (place[None, :] == (place % width * LAGS + place // width)[:, None]).astype(jnp.bfloat16)
    scale = float(count * spectra.shape[1] * freqs) ** (-0.5)
    result = None
    for slot in range(SLOTS):
        result = finish(pair_count, spread, mine, came[:1] + came[1 + slot : 2 + slot], slot, count, piece, scale, result)
    return result


def solution(mesh):
    in_specs = (P("src", "seg", None, None), P("src", None), P("src"))
    out_specs = P("src", "seg", None)
    return jax.shard_map(shards, mesh=mesh, in_specs=in_specs, out_specs=out_specs, check_vma=False)
```

```python
import functools

import jax
import jax.numpy as jnp
from jax import lax
from jax.experimental import pallas as pl
from jax.experimental.pallas import tpu as pltpu
from jax.sharding import PartitionSpec as P

LAGS = 6
REACH = 4
SLOTS = 2
WINDOW = 6
LANES = 128
VMEM = 56 * 1024 * 1024


def routes(axis, move):
    size = lax.axis_size(axis)
    return [(i, move(i)) for i in range(size) if 0 <= move(i) < size]


def to_pair(value):
    return lax.ppermute(value, "src", routes("src", lambda d: d ^ 1))


def to_row(value):
    return lax.ppermute(value, "src", routes("src", lambda d: d ^ 2))


def to_below(value):
    return lax.ppermute(value, "src", routes("src", lambda d: d - REACH))


def lag_tables(freqs, lags):
    freq = jnp.arange(freqs, dtype=jnp.int32)
    lagval = jnp.arange(lags, dtype=jnp.int32) - lags // 2
    phase = lagval[:, None] * freq[None, :] % (2 * freqs)
    theta = phase.astype(jnp.float32) * (jnp.pi / freqs)
    return (jnp.cos(theta), jnp.sin(theta))


def rotate_into(x_ref, real, imag, table, rows, row, cols, half):
    height = real.shape[0]
    other = pl.ds(half + cols, real.shape[1])
    here = pl.ds(cols, real.shape[1])

    def put(lag, first, second):
        at = pl.ds(lag * rows + row, height)
        x_ref[at, here] = first.astype(jnp.bfloat16)
        x_ref[at, other] = second.astype(jnp.bfloat16)

    put(3, real, imag)
    for plus, minus, row_c in ((0, None, 0), (4, 2, 1), (5, 1, 2)):
        cos, sin = table(row_c), table(row_c + 3)
        rc, im_s, ic, rs = real * cos, imag * sin, imag * cos, real * sin
        put(plus, rc - im_s, ic + rs)
        if minus is not None:
            put(minus, rc + im_s, ic - rs)


def stage_tiles(stage):
    return [(a, stage) for a in range(stage)] + [(stage, b) for b in range(stage + 1)]


def corr_kernel(count, stage, first, sets, layout, meta, table, *refs):
    parts = stage + 1
    arrays = 1 + max(item[0] for items in layout for item in items)
    blocks, outs = refs[:arrays], refs[arrays:-4]
    left, right, x_ref, sems = refs[-4:]
    at = pl.program_id(0)
    now = lax.rem(at, 2)
    half = left.shape[3]
    size = left.shape[2] // parts
    piece = size // count

    def copy(item, buffer, p, side):
        ref, source, start, rows = item
        span = pl.ds(start, rows)
        target = left.at[buffer, p, span] if side == 0 else right.at[buffer, span, pl.ds(p * half, half)]
        return pltpu.make_async_copy(blocks[ref].at[p, pl.ds(source, rows)], target, sems.at[side, buffer])

    def fetch(which, buffer):
        for side in range(2):
            name = meta[2 * (first + which) + side]
            for k, items in enumerate(layout):

                @pl.when(name == k)
                def _():
                    for item in items:
                        for p in range(2):
                            copy(item, buffer, p, side).start()

    @pl.when(at == 0)
    def _():
        fetch(0, 0)

    @pl.when(at + 1 < pl.num_programs(0))
    def _():
        fetch(at + 1, 1 - now)

    for side in range(2):
        target = left.at[now] if side == 0 else right.at[now]
        pltpu.make_async_copy(target, target, sems.at[side, now]).wait()

    wide, high = 256, 16
    for c in range(parts):
        for k in range(count):
            base = c * size + lax.rem(meta[8] + k, count) * piece
            block = (c * count + k) * LAGS * piece
            for cols in range(0, half, wide):
                for step in range(0, piece, high):
                    src = pl.ds(pl.multiple_of(base + step, high), high)
                    real = left[now, 0, src, pl.ds(cols, wide)].astype(jnp.float32)
                    imag = left[now, 1, src, pl.ds(cols, wide)].astype(jnp.float32)
                    look = lambda r: table[pl.ds(r, 1), pl.ds(cols, wide)]
                    rotate_into(x_ref, real, imag, look, piece, block + step, cols, half)
    product = lax.dot_general(
        x_ref[...], right[now], (((1,), (1,)), ((), ())), preferred_element_type=jnp.float32
    )
    for n, (which, slot, tiles) in enumerate(sets):

        @pl.when((at // SLOTS == which) if slot is None else (at == which * SLOTS + slot))
        def _():
            for k in range(count):
                for tile, (a, b) in enumerate(tiles):
                    block = (a * count + k) * LAGS * piece
                    out = product[block : block + LAGS * piece, b * size : (b + 1) * size]
                    outs[n * count + k][0, :, tile * piece : (tile + 1) * piece] = out.reshape(LAGS, piece, size)


def correlate(meta, table, sources, count, stage, width, first, sets):
    size, half, parts = width, sources[0][0][0].shape[2], stage + 1
    piece = size // count
    layout, blocks = [], []
    for spans in sources:
        items, start = [], 0
        for array, source, rows in spans:
            rows = min(rows, parts * size - start)
            if rows > 0:
                if not any(array is block for block in blocks):
                    blocks.append(array)
                at = [array is block for block in blocks].index(True)
                items.append((at, source, start, rows))
                start += rows
        layout.append(tuple(items))
    shapes = [
        (SLOTS if slot is None else 1, LAGS, len(tiles) * piece, size) for _, slot, tiles in sets for _ in range(count)
    ]
    steps = SLOTS * (1 + max(which for which, _, _ in sets))
    outs = pl.pallas_call(
        functools.partial(corr_kernel, count, stage, first, sets, tuple(layout)),
        out_shape=[jax.ShapeDtypeStruct(shape, jnp.float32) for shape in shapes],
        grid=(steps,),
        in_specs=[pl.BlockSpec(memory_space=pltpu.SMEM), pl.BlockSpec(memory_space=pltpu.VMEM)]
        + [pl.BlockSpec(memory_space=pl.ANY)] * len(blocks),
        out_specs=[
            pl.BlockSpec((1,) + shape[1:], lambda s, n=sets[n // count][0], top=shape[0] - 1: (jnp.clip(s - n * SLOTS, 0, top), 0, 0, 0))
            for n, shape in enumerate(shapes)
        ],
        scratch_shapes=[
            pltpu.VMEM((2, 2, parts * size, half), jnp.bfloat16),
            pltpu.VMEM((2, parts * size, 2 * half), jnp.bfloat16),
            pltpu.VMEM((parts * LAGS * size, 2 * half), jnp.bfloat16),
            pltpu.SemaphoreType.DMA((2, 2)),
        ],
        compiler_params=pltpu.CompilerParams(vmem_limit_bytes=VMEM),
        cost_estimate=pl.CostEstimate(flops=10**13, bytes_accessed=10**10, transcendentals=0),
    )(meta, table, *blocks)
    return [outs[n * count : (n + 1) * count] for n in range(len(sets))]


def finish_kernel(count, piece, layout, slot, scale, pair_count, spread, *refs):
    out = refs[-1]
    stages = len(layout)
    tiles = [(stage, t, a, b) for stage in range(stages) for t, (a, b) in enumerate(stage_tiles(stage))]
    own, came = refs[: len(tiles) // 2], refs[len(tiles) // 2 :]
    high, low = [], []
    for n, (stage, t, _, _) in enumerate(tiles):
        at = slice(t * piece, (t + 1) * piece)
        rows = slice(n % 2 * piece, (n % 2 + 1) * piece)
        lags = [own[n // 2][0, lag, rows] + came[ref][0, lag - first, at] for lag, (ref, first) in enumerate(layout[stage])]
        total = jnp.concatenate(lags, axis=1)
        top = total.astype(jnp.bfloat16)
        high.append(top)
        low.append((total - top.astype(jnp.float32)).astype(jnp.bfloat16))
    moved = jnp.dot(jnp.concatenate(high + low, axis=0), spread[...], preferred_element_type=jnp.float32)
    keep = slot < pair_count[0]
    run = piece * LAGS
    for n, (_, _, a, b) in enumerate(tiles):
        m = n + len(tiles)
        both = (moved[n * piece : (n + 1) * piece] + moved[m * piece : (m + 1) * piece]) * scale
        both = jnp.where(keep, both, jnp.zeros_like(both))
        for seg in range(count):
            col = (seg * stages + b) * run
            out[0, a * piece : (a + 1) * piece, col : col + run] = both[:, seg * run : (seg + 1) * run]


def finish(pair_count, spread, own, came, slot, count, piece, scale, result):
    stages = len(came)
    arrays, layout = [*own], []
    for pieces in came:
        layout.append([])
        for first, array in pieces:
            layout[-1] += [(len(arrays) - len(own), first)] * array.shape[1]
            arrays.append(array)
    shape = (SLOTS, stages * piece, stages * piece * count * LAGS)
    specs = [pl.BlockSpec((1,) + x.shape[1:], lambda i, at=min(slot, x.shape[0] - 1): (at, 0, 0, 0)) for x in arrays]
    more = [] if result is None else [result]
    return pl.pallas_call(
        functools.partial(finish_kernel, count, piece, layout, slot, scale),
        out_shape=jax.ShapeDtypeStruct(shape, jnp.float32),
        grid=(1,),
        in_specs=[pl.BlockSpec(memory_space=pltpu.SMEM), pl.BlockSpec(memory_space=pltpu.VMEM)]
        + specs
        + [pl.BlockSpec(memory_space=pl.ANY)] * len(more),
        out_specs=pl.BlockSpec((1,) + shape[1:], lambda i: (slot, 0, 0)),
        input_output_aliases={2 + len(arrays): 0} if more else {},
        compiler_params=pltpu.CompilerParams(vmem_limit_bytes=VMEM),
        cost_estimate=pl.CostEstimate(flops=1, bytes_accessed=1, transcendentals=0),
    )(pair_count, spread, *arrays, *more)


def after(value, *done):
    return lax.optimization_barrier((value, *done))[0] if done else value


def over_segments(shares, count):
    parts = [shares[0]]
    for k in range(1, count):
        parts.append(lax.ppermute(shares[k], "seg", routes("seg", lambda i: (i + k) % count)))
    return parts


def shards(spectra, pairs, pair_count):
    blk, freqs = spectra.shape[0], spectra.shape[3]
    half = freqs // 2
    count = lax.axis_size("seg")
    me = lax.axis_index("src")
    seg = lax.axis_index("seg")
    side, row = me & 1, (me >> 1) & 1
    stages = 2
    width = blk // stages
    piece = width // count

    rows = spectra.reshape(count, stages, piece, 2, freqs).transpose(3, 1, 0, 2, 4).reshape(2, blk, freqs)
    rows = lax.optimization_barrier(rows)
    own, theirs = [lax.dynamic_slice_in_dim(rows, which * half, half, 2) for which in (side, 1 - side)]

    sources = [[] for _ in range(WINDOW)]
    along, beside = [], []
    with jax.named_scope("swap"):
        swapped = [to_pair(theirs[:, c * width : (c + 1) * width]) for c in range(stages)]
    for c in range(stages):
        for kind in range(2):
            block = (own[:, c * width : (c + 1) * width], swapped[c])[kind]
            with jax.named_scope(f"along_{kind}_{c}"):
                along.append(to_below(after(block, *along[-2:-1])))
            if len(along) == 2:
                with jax.named_scope("pairs"):
                    named = to_pair(after(pairs, along[1]))
            with jax.named_scope(f"beside_{kind}_{c}"):
                beside.append(to_row(after(jnp.where(row == 1, block, along[-1]), *beside[-2:-1])))
            for group, array in enumerate((block, beside[-1], along[-1])):
                sources[2 * group + kind].append((array, 0, width))

    named = jnp.clip(jnp.concatenate([named, pairs], axis=0) - (me & ~1), 0, WINDOW - 1)
    local = 2 * (named >> 1) + ((named & 1) ^ side)
    meta = jnp.concatenate([local.reshape(-1), seg[None]]).astype(jnp.int32)
    meta = after(meta, along[-1])

    cosine, sine = lag_tables(freqs, LAGS)
    table = jnp.concatenate([part[at : at + 1] for part in (cosine, sine) for at in (0, 4, 5)] + [cosine[:2]], axis=0)
    table = lax.dynamic_slice_in_dim(table, side * half, half, 1)

    here, back = [], []

    def over_all(shares, name):
        with jax.named_scope(f"segments_{name}"):
            return sum(over_segments(shares, count))

    def exchange(total, name):
        with jax.named_scope(f"partner_stacks_{name}"):
            return to_pair(total)

    (partner,) = correlate(meta, table, sources, count, 0, width, 0, ((0, None, stage_tiles(0)),))
    total = over_all(partner, "0")
    came = [exchange(total, "0")]
    meta = after(meta, total)
    tiles = stage_tiles(1)
    groups = correlate(meta, table, sources, count, 1, width, 0, tuple((0, slot, tiles) for slot in range(SLOTS)))
    totals = [over_all([after(x, came[0]) for x in shares], f"1_{slot}") for slot, shares in enumerate(groups)]
    came.append(exchange(totals[0], "1_0"))
    meta = after(meta, *totals)
    tiles = stage_tiles(0) + tiles
    groups = correlate(meta, table, sources, count, 1, width, SLOTS, tuple((0, None, tiles[n : n + 2]) for n in range(0, len(tiles), 2)))
    half_lags = LAGS // 2
    total = after(totals[1], groups[0][0])
    halves = [exchange(total[:, :half_lags], "1_1a"), exchange(after(total[:, half_lags:], came[1]), "1_1b")]
    arrived = [[(0, came[0])], [(0, came[1])]], [[(0, came[0])], [(0, halves[0]), (half_lags, halves[1])]]
    mine = [over_all(shares, f"own_{n}") for n, shares in enumerate(groups)]
    place = jnp.arange(LAGS * width)
    spread = (place[None, :] == (place % width * LAGS + place // width)[:, None]).astype(jnp.bfloat16)
    scale = float(count * spectra.shape[1] * freqs) ** (-0.5)
    result = None
    for slot in range(SLOTS):
        result = finish(pair_count, spread, mine, arrived[slot], slot, count, piece, scale, result)
    return result


def solution(mesh):
    in_specs = (P("src", "seg", None, None), P("src", None), P("src"))
    out_specs = P("src", "seg", None)
    return jax.shard_map(shards, mesh=mesh, in_specs=in_specs, out_specs=out_specs, check_vma=False)
```
